512 devices in a mesh: layer: 8 (over x_lo, y), ex: 64 (over z, x_hi, core).
Axes of the slice: x: 4 (x_hi: 2, x_lo: 2; x = x_hi * 2 + x_lo), y: 4, z: 16, core: 2. Of those that a mesh axis runs over, the one named last changes fastest.
Arguments:
- queries: bfloat16 [8, 512, 4096], P('layer', 'ex'), may hold values from -6 to 6
- fisher: bfloat16 [8, 4096, 4096], P('layer', None, 'ex'), may hold values from -0.2 to 3, as said below
- train_grads: bfloat16 [8, 24576, 4096], P('layer', 'ex'), may hold values from -0.09375 to 0.09375
Outputs:
- scores: float32 [512, 24576], P('layer', 'ex')
The draws below stay inside these ranges and needn't reach their ends.
Inputs may be any that keep to these rules, and one draw needn't show every extreme that they name: fisher[l] is symmetric for every layer l.
All inputs are finite; a program needn't handle non-finite values.
Results may differ from the reference program's by a relative error of at most 0.0029.
Values may be sent and summed in bfloat16 or wider, within the bound.
No kernel may reach another device: no remote copies, remote signals or barrier semaphores. Data moves between devices by JAX's collectives and lax.ppermute only.
A program may use at most 64 MiB of HBM per device.

```python
import jax
import jax.numpy as jnp
from jax import lax

W = 4096
NQ = 512
LAYERS = 8
EXAMPLES = 24576


def draw_fisher(key, part):
    key = jax.random.fold_in(key, 5)
    first, second = jax.random.split(key)
    offdiag = jnp.clip(jax.random.normal(first, (LAYERS, W, W), jnp.float32), -3.5, 3.5)
    diagonal = jax.random.uniform(second, (LAYERS, W), jnp.float32, 1.0, 2.0)
    sym = (offdiag + jnp.swapaxes(offdiag, 1, 2)) * (0.35 / jnp.sqrt(jnp.float32(W)))
    rowidx = lax.broadcasted_iota(jnp.int32, (W, W), 0)
    colidx = lax.broadcasted_iota(jnp.int32, (W, W), 1)
    identity = (rowidx == colidx).astype(jnp.float32)[None]
    matrix = sym * (1.0 - identity) + diagonal[:, :, None] * identity
    return matrix.astype(jnp.bfloat16)


def level_of(rng, extent, pieces, smallest, top_value):
    level, own = 1.0, jax.random.fold_in(rng, 6)
    for position, shards_of in pieces:
        steps = jnp.exp(jax.random.uniform(jax.random.fold_in(own, position), (shards_of,), jnp.float32, smallest / len(pieces), top_value / len(pieces)))
        level = level * jnp.repeat(steps, extent[position] // shards_of).reshape([-1 if axis == position else 1 for axis in range(len(extent))])
    return level


def normal_values(stream_key, dims, spread, most, shards=(), held_as=jnp.bfloat16):
    loudness = level_of(stream_key, dims, shards, -0.22, 0.18) if shards else 1.0
    result = jax.random.normal(stream_key, dims, jnp.float32) * spread * loudness
    return jnp.minimum(jnp.maximum(result, -most), most).astype(held_as)


def setup_inputs(seed: int = 0) -> dict:
    keys = jax.random.split(jax.random.key(seed), 4)
    queries = normal_values(keys[0], (LAYERS, NQ, W), 1.0, 6.0, ((0, 8), (1, 64)))
    fisher = draw_fisher(jax.random.fold_in(keys[3], 71), 0)
    train_grads = normal_values(keys[2], (LAYERS, EXAMPLES, W), W ** -0.5, 0.09375, ((0, 8), (1, 64)))
    return dict(queries=queries, fisher=fisher, train_grads=train_grads)


def reference(queries, fisher, train_grads):
    total = jnp.zeros((NQ, EXAMPLES), jnp.float32)
    for layer in range(LAYERS):
        pre = jnp.dot(queries[layer], fisher[layer], preferred_element_type=jnp.float32).astype(jnp.bfloat16)
        total = total + lax.dot_general(pre, train_grads[layer], (((1,), (1,)), ((), ())), preferred_element_type=jnp.float32)
    return total
```

```python
import jax
import jax.numpy as jnp
from jax import lax
from jax.sharding import Mesh, PartitionSpec as P

TOP = 14.0


def exponent_of(peak):
    return jnp.clip(jnp.floor(jnp.log2(jnp.maximum(peak, 1e-37))), -100.0, 100.0)


def on_device(queries, fisher, train_grads):
    width = queries.shape[2]
    fisher_slab = lax.all_gather(fisher[0].T, ("xh", "c"), axis=0, tiled=True)
    train_chip = lax.all_gather(train_grads[0], "c", axis=0, tiled=True)

    own = queries[0].astype(jnp.float32)
    exponent = exponent_of(jnp.max(jnp.abs(own), axis=1, keepdims=True))
    scaled = (own * jnp.exp2(TOP - exponent)).astype(jnp.float16)
    tail = jnp.broadcast_to(exponent, (own.shape[0], 128)).astype(jnp.float16)
    rows = lax.all_gather(jnp.concatenate([scaled, tail], axis=1), "z", axis=0, tiled=True)
    back = jnp.exp2(rows[:, width : width + 1].astype(jnp.float32) - TOP)
    pre = lax.dot_general(
        rows[:, :width].astype(jnp.bfloat16), fisher_slab, (((1,), (1,)), ((), ())),
        preferred_element_type=jnp.float32,
    )
    pre = (pre * back).astype(jnp.bfloat16)

    slots = lax.axis_size("z")
    pre = lax.all_gather(pre.reshape(slots, own.shape[0], -1), "xh", axis=1)
    pre = pre.reshape(-1, pre.shape[-1]).astype(jnp.float32)
    height, span = pre.shape
    exponent = exponent_of(jnp.max(jnp.abs(pre)))
    scaled = (pre * jnp.exp2(TOP - exponent)).astype(jnp.float16)
    tail = jnp.broadcast_to(exponent, (8, span)).astype(jnp.float16)
    blocks = lax.all_gather(jnp.concatenate([scaled, tail], axis=0), "z", axis=0)
    back = jnp.exp2(blocks[:, height : height + 1, :1].astype(jnp.float32) - TOP)
    whole = (blocks[:, :height].astype(jnp.float32) * back).astype(jnp.bfloat16)
    whole = jnp.swapaxes(whole, 0, 1).reshape(height, width)
    partial_value = lax.dot_general(
        whole, train_chip, (((1,), (1,)), ((), ())), preferred_element_type=jnp.float32
    )

    layers = lax.axis_size("layer")
    parts = lax.all_to_all(partial_value.reshape(layers, height // layers, -1), "layer", 0, 0)
    total = jnp.sum(parts, axis=0)
    group = own.shape[0]
    total = total.reshape(-1, group, 2, total.shape[-1] // 2)
    total = lax.all_to_all(total, "c", 2, 1)
    return total.reshape(-1, total.shape[-1])


def solution(mesh):
    layers, spread = mesh.devices.shape
    fine = Mesh(mesh.devices.reshape(layers, spread // 4, 2, 2), ("layer", "z", "xh", "c"))
    ex = ("z", "xh", "c")
    in_specs = (P("layer", ex, None), P("layer", None, ex), P("layer", ex, None))
    return jax.shard_map(
        on_device, mesh=fine, in_specs=in_specs, out_specs=P("layer", ex), check_vma=False
    )
```

```python
import jax
import jax.numpy as jnp
from jax import lax
from jax.sharding import Mesh, PartitionSpec as P

TOP = 14.0
SWAP = [(0, 1), (1, 0)]


def exponent_of(peak):
    return jnp.clip(jnp.floor(jnp.log2(jnp.maximum(peak, 1e-37))), -100.0, 100.0)


def on_device(queries, fisher, train_grads):
    width = queries.shape[2]
    mine = fisher[0].T
    fisher_slab = jnp.concatenate(
        [
            mine,
            lax.ppermute(mine, "c", SWAP),
            lax.ppermute(mine, "xh", SWAP),
            lax.ppermute(mine, ("xh", "c"), [(0, 3), (3, 0), (1, 2), (2, 1)]),
        ]
    )
    train_other = lax.ppermute(train_grads[0], "c", SWAP)

    own = queries[0].astype(jnp.float32)
    exponent = exponent_of(jnp.max(jnp.abs(own), axis=1, keepdims=True))
    scaled = (own * jnp.exp2(TOP - exponent)).astype(jnp.float16)
    tail = jnp.broadcast_to(exponent, (own.shape[0], 128)).astype(jnp.float16)
    rows = lax.all_gather(jnp.concatenate([scaled, tail], axis=1), "z", axis=0, tiled=True)
    back = jnp.exp2(rows[:, width : width + 1].astype(jnp.float32) - TOP)
    pre = lax.dot_general(
        rows[:, :width].astype(jnp.bfloat16), fisher_slab, (((1,), (1,)), ((), ())),
        preferred_element_type=jnp.float32,
    )
    pre = (pre * back).astype(jnp.bfloat16)
    first_chip, first_core = lax.axis_index("xh") == 0, lax.axis_index("c") == 0
    pre = pre.reshape(-1, 2, 2, pre.shape[-1] // 4)
    pre = jnp.where(first_core, pre, pre[:, :, ::-1])
    pre = jnp.where(first_chip, pre, pre[:, ::-1]).reshape(pre.shape[0], -1)

    slots = lax.axis_size("z")
    pre = pre.reshape(slots, 1, own.shape[0], -1)
    got = lax.ppermute(pre, "xh", SWAP)
    pre = jnp.where(first_chip, jnp.concatenate([pre, got], axis=1), jnp.concatenate([got, pre], axis=1))
    pre = pre.reshape(-1, pre.shape[-1]).astype(jnp.float32)
    height, span = pre.shape
    exponent = exponent_of(jnp.max(jnp.abs(pre)))
    scaled = (pre * jnp.exp2(TOP - exponent)).astype(jnp.float16)
    tail = jnp.broadcast_to(exponent, (8, span)).astype(jnp.float16)
    blocks = lax.all_gather(jnp.concatenate([scaled, tail], axis=0), "z", axis=0)
    back = jnp.exp2(blocks[:, height : height + 1, :1].astype(jnp.float32) - TOP)
    whole = (blocks[:, :height].astype(jnp.float32) * back).astype(jnp.bfloat16)
    whole = jnp.swapaxes(whole, 0, 1).reshape(height, width)
    by_own = lax.dot_general(whole, train_grads[0], (((1,), (1,)), ((), ())), preferred_element_type=jnp.float32)
    by_other = lax.dot_general(whole, train_other, (((1,), (1,)), ((), ())), preferred_element_type=jnp.float32)

    layers, group = lax.axis_size("layer"), own.shape[0]
    parts = jnp.concatenate([by_own, by_other], axis=1).reshape(layers, height // layers, -1)
    total = jnp.sum(lax.all_to_all(parts, "layer", 0, 0), axis=0)
    keep, give = jnp.split(total.reshape(-1, 1, group, total.shape[-1]), 2, axis=-1)
    got = lax.ppermute(give, "c", SWAP)
    both = jnp.where(first_core, jnp.concatenate([keep, got], axis=1), jnp.concatenate([got, keep], axis=1))
    return both.reshape(-1, both.shape[-1])


def solution(mesh):
    layers, spread = mesh.devices.shape
    fine = Mesh(mesh.devices.reshape(layers, spread // 4, 2, 2), ("layer", "z", "xh", "c"))
    ex = ("z", "xh", "c")
    in_specs = (P("layer", ex, None), P("layer", None, ex), P("layer", ex, None))
    return jax.shard_map(
        on_device, mesh=fine, in_specs=in_specs, out_specs=P("layer", ex), check_vma=False
    )
```

```python
import functools

import jax
import jax.numpy as jnp
from jax import lax
from jax.experimental import pallas as pl
from jax.experimental.pallas import tpu as pltpu
from jax.sharding import Mesh, PartitionSpec as P

TOP = 14.0
AXES = ("layer", "z", "xh", "c")
SWAP = [(0, 1), (1, 0)]
CYCLE = [(1, 0), (0, 2), (2, 3), (3, 1)]
CROSS = [(1, 2), (2, 1)]
NT = (((1,), (1,)), ((), ()))


def exponent_of(peak):
    return jnp.clip(jnp.floor(jnp.log2(jnp.maximum(peak, 1e-37))), -100.0, 100.0)


def gather_z(x, groups):
    return lax.all_gather(x, AXES, axis=0, axis_index_groups=groups)


def add_blocks(total, blocks, train, side):
    for z in range(0, blocks.shape[0], 2):
        first = pl.multiple_of((2 * z + side) * 128, 128)
        second = pl.multiple_of((2 * z + 3 - side) * 128, 128)
        left = jnp.concatenate([blocks[z], blocks[z + 1]], axis=1)
        right = jnp.concatenate([train[:, pl.ds(first, 128)], train[:, pl.ds(second, 128)]], axis=1)
        total = total + lax.dot_general(left, right, NT, preferred_element_type=jnp.float32)
    return total


def side_of():
    return lax.rem(lax.axis_index("c") + lax.axis_index("z"), 2)


def first_kernel(own, train, out):
    out[...] = add_blocks(jnp.zeros(out.shape, jnp.float32), own, train, side_of())


def second_kernel(begun, own, other, train, train_got, out):
    side, chip = side_of(), lax.axis_index("xh")
    layers, _, rows, _ = out.shape
    here = add_blocks(begun[...], other, train, 1 - side)
    for layer in range(layers):
        out[layer, chip] = here[layer * rows : (layer + 1) * rows]
    there = add_blocks(jnp.zeros(begun.shape, jnp.float32), own, train_got, side)
    there = add_blocks(there, other, train_got, 1 - side)
    for layer in range(layers):
        out[layer, 1 - chip] = there[layer * rows : (layer + 1) * rows]


def in_vmem(kernel, out_shape, *operands):
    flops = 2 * sum(x.size for x in operands[:1]) * operands[-1].shape[0]
    spec = pl.BlockSpec(memory_space=pltpu.VMEM)
    return pl.pallas_call(
        kernel,
        out_shape=out_shape,
        in_specs=[spec] * len(operands),
        out_specs=spec,
        compiler_params=pltpu.CompilerParams(vmem_limit_bytes=40 * 2**20),
        cost_estimate=pl.CostEstimate(flops=flops, bytes_accessed=2**20, transcendentals=0),
    )(*operands)


def on_device(groups, queries, fisher, train_grads):
    width, group = queries.shape[2], queries.shape[1]
    layers, slots = lax.axis_size("layer"), lax.axis_size("z")
    chip, core, side = lax.axis_index("xh"), lax.axis_index("c"), side_of()
    train = train_grads[0]

    mine = fisher[0].T
    cycled = lax.ppermute(mine, ("xh", "c"), CYCLE)
    crossed = lax.ppermute(mine, ("xh", "c"), CROSS)
    train_got = lax.ppermute(train, "xh", SWAP)

    wide = queries[0].astype(jnp.float32)
    exponent = exponent_of(jnp.max(jnp.abs(wide), axis=1, keepdims=True))
    scaled = (wide * jnp.exp2(TOP - exponent)).astype(jnp.float16)
    tail = jnp.broadcast_to(exponent, (group, 128)).astype(jnp.float16)
    rows = gather_z(jnp.concatenate([scaled, tail], axis=1), groups).reshape(slots * group, width + 128)
    rows_got = lax.ppermute(rows, "c", SWAP)

    kept = jnp.where(chip == core, mine, crossed)
    low = jnp.where(chip == 0, kept, cycled)
    high = jnp.where(chip == 0, cycled, kept)
    columns = jnp.concatenate([low, high], axis=0)

    def product(part):
        back = jnp.exp2(part[:, width : width + 1].astype(jnp.float32) - TOP)
        value = lax.dot_general(part[:, :width].astype(jnp.bfloat16), columns, NT, preferred_element_type=jnp.float32)
        return (value * back).astype(jnp.bfloat16).reshape(slots, 1, group, columns.shape[0])

    near, far = product(rows), product(rows_got)
    flip = (lax.broadcasted_iota(jnp.int32, (slots, 1, 1, 1), 0) + side) % 2 == 0
    pre = jnp.concatenate([jnp.where(flip, near, far), jnp.where(flip, far, near)], axis=1)
    height, span = slots * 2 * group, columns.shape[0]
    pre = pre.reshape(height, span).astype(jnp.float32)

    exponent = exponent_of(jnp.max(jnp.abs(pre)))
    scaled = (pre * jnp.exp2(TOP - exponent)).astype(jnp.float16)
    tail = jnp.broadcast_to(exponent, (8, span)).astype(jnp.float16)
    blocks = gather_z(jnp.concatenate([scaled, tail], axis=0), groups)
    back = jnp.exp2(blocks[:, height : height + 1, :1].astype(jnp.float32) - TOP)
    own = (blocks[:, :height].astype(jnp.float32) * back).astype(jnp.bfloat16)
    other = lax.ppermute(own, "c", SWAP)
    begun = in_vmem(first_kernel, jax.ShapeDtypeStruct((height, train.shape[0]), jnp.float32), own, train)
    parts_shape = jax.ShapeDtypeStruct((layers, 2, height // layers, train.shape[0]), jnp.float32)
    parts = in_vmem(second_kernel, parts_shape, begun, own, other, train, train_got)

    parts = lax.all_to_all(parts.reshape(2 * layers, height // layers, -1), ("layer", "xh"), 0, 0)
    total = jnp.sum(parts.reshape(layers, 2, -1, 2 * group, parts.shape[-1]), axis=0)
    return jnp.swapaxes(total, 0, 1).reshape(-1, parts.shape[-1])


def solution(mesh):
    layers, spread = mesh.devices.shape
    slots = spread // 4
    fine = Mesh(mesh.devices.reshape(layers, slots, 2, 2), AXES)
    groups = [
        [layer * spread + 4 * z + 2 * chip + (side + z) % 2 for z in range(slots)]
        for layer in range(layers)
        for chip in range(2)
        for side in range(2)
    ]
    ex = ("z", "xh", "c")
    in_specs = (P("layer", ex, None), P("layer", None, ex), P("layer", ex, None))
    return jax.shard_map(
        functools.partial(on_device, groups),
        mesh=fine,
        in_specs=in_specs,
        out_specs=P("layer", ex),
        check_vma=False,
    )
```

```python
import functools

import jax
import jax.numpy as jnp
from jax import lax
from jax.experimental import pallas as pl
from jax.experimental.pallas import tpu as pltpu
from jax.sharding import Mesh, PartitionSpec as P

TOP = 14.0
AXES = ("layer", "z", "xh", "c")
SWAP = [(0, 1), (1, 0)]
CYCLE = [(1, 0), (0, 2), (2, 3), (3, 1)]
CROSS = [(1, 2), (2, 1)]
NT = (((1,), (1,)), ((), ()))


def exponent_of(peak):
    return jnp.clip(jnp.floor(jnp.log2(jnp.maximum(peak, 1e-37))), -100.0, 100.0)


def gather_z(x, groups):
    return lax.all_gather(x, AXES, axis=0, axis_index_groups=groups)


def add_blocks(total, blocks, train, side, begin=0):
    for z in range(0, train.shape[1] // 256, 2):
        first = pl.multiple_of((2 * z + side) * 128, 128)
        second = pl.multiple_of((2 * z + 3 - side) * 128, 128)
        left = jnp.concatenate([blocks[begin + z], blocks[begin + z + 1]], axis=1)
        right = jnp.concatenate([train[:, pl.ds(first, 128)], train[:, pl.ds(second, 128)]], axis=1)
        total = total + lax.dot_general(left, right, NT, preferred_element_type=jnp.float32)
    return total


def side_of():
    return lax.rem(lax.axis_index("c") + lax.axis_index("z"), 2)


def columns_of(mine, cycled, crossed):
    chip, core = lax.axis_index("xh"), lax.axis_index("c")
    kept = jnp.where(chip == core, mine[...], crossed[...])
    low = jnp.where(chip == 0, kept, cycled[...])
    high = jnp.where(chip == 0, cycled[...], kept)
    return jnp.concatenate([low, high], axis=0)


def rounded_product(rows, columns):
    value = lax.dot_general(rows[...], columns, NT, preferred_element_type=jnp.float32)
    return value.astype(jnp.bfloat16).astype(jnp.float32)


def near_kernel(rows, mine, cycled, crossed, out):
    out[...] = rounded_product(rows, columns_of(mine, cycled, crossed))


def chunk_kernel(near, rows, mine, cycled, crossed, out, order):
    side = side_of()
    far = rounded_product(rows, columns_of(mine, cycled, crossed))
    height = order.shape[0]
    group = out.shape[0] - height
    for z in range(height // (2 * group)):
        first = lax.rem(side + z, 2)
        piece = slice(z * group, (z + 1) * group)
        order[pl.ds(pl.multiple_of((2 * z + first) * group, group), group)] = near[piece]
        order[pl.ds(pl.multiple_of((2 * z + 1 - first) * group, group), group)] = far[piece]
    value = order[...]
    peak = jnp.max(jnp.max(jnp.abs(value), axis=0, keepdims=True), axis=1, keepdims=True)
    exponent = exponent_of(peak)
    tail = jnp.broadcast_to(exponent, (group, out.shape[1]))
    out[...] = jnp.concatenate([value * jnp.exp2(TOP - exponent), tail], axis=0)


def first_kernel(own, train, out):
    out[...] = add_blocks(jnp.zeros(out.shape, jnp.float32), own, train, side_of())


def second_kernel(begun, own, other, train, early, late, out):
    side, chip = side_of(), lax.axis_index("xh")
    layers, _, rows, _ = out.shape
    here = add_blocks(begun[...], other, train, 1 - side)
    for layer in range(layers):
        out[layer, chip] = here[layer * rows : (layer + 1) * rows]
    there = jnp.zeros(begun.shape, jnp.float32)
    for piece, begin in ((early, 0), (late, early.shape[1] // 256)):
        there = add_blocks(there, own, piece, side, begin)
        there = add_blocks(there, other, piece, 1 - side, begin)
    for layer in range(layers):
        out[layer, 1 - chip] = there[layer * rows : (layer + 1) * rows]


def in_vmem(kernel, out_shape, *operands, scratch=()):
    flops = 2 * operands[0].size * operands[1].shape[0]
    spec = pl.BlockSpec(memory_space=pltpu.VMEM)
    return pl.pallas_call(
        kernel,
        out_shape=out_shape,
        in_specs=[spec] * len(operands),
        out_specs=spec,
        scratch_shapes=scratch,
        compiler_params=pltpu.CompilerParams(vmem_limit_bytes=40 * 2**20),
        cost_estimate=pl.CostEstimate(flops=flops, bytes_accessed=2**20, transcendentals=0),
    )(*operands)


def on_device(groups, queries, fisher, train_grads):
    width, group = queries.shape[2], queries.shape[1]
    layers, slots = lax.axis_size("layer"), lax.axis_size("z")
    train = train_grads[0]
    cut = 256 * (slots * 3 // 16 * 2 or 2)

    mine = fisher[0].T
    cycled = lax.ppermute(mine, ("xh", "c"), CYCLE)
    crossed = lax.ppermute(mine, ("xh", "c"), CROSS)
    early = lax.ppermute(train[:, :cut], "xh", SWAP)
    late = lax.ppermute(train[:, cut:], "xh", SWAP)

    wide = queries[0].astype(jnp.float32)
    exponent = exponent_of(jnp.max(jnp.abs(wide), axis=1, keepdims=True))
    scaled = (wide * jnp.exp2(TOP - exponent)).astype(jnp.float16)
    tail = jnp.broadcast_to(exponent, (group, 128)).astype(jnp.float16)
    rows = gather_z(jnp.concatenate([scaled, tail], axis=1), groups).reshape(slots * group, width + 128)
    rows, cycled, crossed = lax.optimization_barrier((rows, cycled, crossed))
    blocks_of_fisher = (mine, cycled, crossed)
    back = jnp.exp2(rows[:, width : width + 1].astype(jnp.float32) - TOP)
    rows = (rows[:, :width].astype(jnp.float32) * back).astype(jnp.bfloat16)
    rows_got = lax.ppermute(rows, "c", SWAP)

    height, span = slots * 2 * group, 2 * mine.shape[0]
    near = in_vmem(near_kernel, jax.ShapeDtypeStruct((height // 2, span), jnp.float32), rows, *blocks_of_fisher)
    chunk = in_vmem(
        chunk_kernel,
        jax.ShapeDtypeStruct((height + group, span), jnp.float32),
        near,
        rows_got,
        *blocks_of_fisher,
        scratch=[pltpu.VMEM((height, span), jnp.float32)],
    )
    chunk, early = lax.optimization_barrier((chunk, early))
    blocks = gather_z(chunk.astype(jnp.float16), groups)
    back = jnp.exp2(blocks[:, height : height + 1, :1].astype(jnp.float32) - TOP)
    own = (blocks[:, :height].astype(jnp.float32) * back).astype(jnp.bfloat16)
    other = lax.ppermute(own, "c", SWAP)
    begun = in_vmem(first_kernel, jax.ShapeDtypeStruct((height, train.shape[0]), jnp.float32), own, train)
    parts_shape = jax.ShapeDtypeStruct((layers, 2, height // layers, train.shape[0]), jnp.float32)
    parts = in_vmem(second_kernel, parts_shape, begun, own, other, train, early, late)

    parts = lax.all_to_all(parts.reshape(2 * layers, height // layers, -1), ("layer", "xh"), 0, 0)
    total = jnp.sum(parts.reshape(layers, 2, -1, 2 * group, parts.shape[-1]), axis=0)
    return jnp.swapaxes(total, 0, 1).reshape(-1, parts.shape[-1])


def solution(mesh):
    layers, spread = mesh.devices.shape
    slots = spread // 4
    fine = Mesh(mesh.devices.reshape(layers, slots, 2, 2), AXES)
    groups = [
        [layer * spread + 4 * z + 2 * chip + (side + z) % 2 for z in range(slots)]
        for layer in range(layers)
        for chip in range(2)
        for side in range(2)
    ]
    ex = ("z", "xh", "c")
    in_specs = (P("layer", ex, None), P("layer", None, ex), P("layer", ex, None))
    return jax.shard_map(
        functools.partial(on_device, groups),
        mesh=fine,
        in_specs=in_specs,
        out_specs=P("layer", ex),
        check_vma=False,
    )
```

```python
import functools

import jax
import jax.numpy as jnp
from jax import lax
from jax.experimental import pallas as pl
from jax.experimental.pallas import tpu as pltpu
from jax.sharding import Mesh, PartitionSpec as P

TOP = 14.0
AXES = ("layer", "z", "xh", "c")
SWAP = [(0, 1), (1, 0)]
NT = (((1,), (1,)), ((), ()))


def exponent_of(peak):
    return jnp.clip(jnp.floor(jnp.log2(jnp.maximum(peak, 1e-37))), -100.0, 100.0)


def gather_z(x, groups):
    return lax.all_gather(x, AXES, axis=0, axis_index_groups=groups)


def side_of():
    return lax.rem(lax.axis_index("c") + lax.axis_index("z"), 2)


def columns_of(mine, got):
    first = lax.axis_index("xh") == 0
    return jnp.concatenate([jnp.where(first, mine[...], got[...]), jnp.where(first, got[...], mine[...])], axis=0)


def rounded_product(rows, columns):
    value = lax.dot_general(rows[...], columns, NT, preferred_element_type=jnp.float32)
    return value.astype(jnp.bfloat16).astype(jnp.float32)


def near_kernel(rows, mine, got, out):
    out[...] = rounded_product(rows, columns_of(mine, got))


def chunk_kernel(near, rows, mine, got, out, order):
    side = side_of()
    far = rounded_product(rows, columns_of(mine, got))
    height = order.shape[0]
    group = out.shape[0] - height
    for z in range(height // (2 * group)):
        first = lax.rem(side + z, 2)
        piece = slice(z * group, (z + 1) * group)
        order[pl.ds(pl.multiple_of((2 * z + first) * group, group), group)] = near[piece]
        order[pl.ds(pl.multiple_of((2 * z + 1 - first) * group, group), group)] = far[piece]
    value = order[...]
    peak = jnp.max(jnp.max(jnp.abs(value), axis=0, keepdims=True), axis=1, keepdims=True)
    exponent = exponent_of(peak)
    tail = jnp.broadcast_to(exponent, (group, out.shape[1]))
    out[...] = jnp.concatenate([value * jnp.exp2(TOP - exponent), tail], axis=0)


def score_kernel(own, other, train, early, late, out):
    side, chip = side_of(), lax.axis_index("xh")
    layers, _, rows, count = out.shape
    half = own.shape[2] // 2
    here = jnp.zeros((own.shape[1], count), jnp.float32)
    there = here
    for z in range(own.shape[0]):
        mixed = lax.rem(side + z, 2) == 0
        one = jnp.where(mixed, own[z], other[z])
        two = jnp.where(mixed, other[z], own[z])
        left = jnp.concatenate([one[:, :half], two[:, :half], one[:, half:], two[:, half:]], axis=1)
        span = left.shape[1]
        piece, begin = (early, z * span) if z * span < early.shape[1] else (late, z * span - early.shape[1])
        right = train[:, z * span : (z + 1) * span]
        here = here + lax.dot_general(left, right, NT, preferred_element_type=jnp.float32)
        right = piece[:, begin : begin + span]
        there = there + lax.dot_general(left, right, NT, preferred_element_type=jnp.float32)
    for layer in range(layers):
        out[layer, chip] = here[layer * rows : (layer + 1) * rows].astype(out.dtype)
        out[layer, 1 - chip] = there[layer * rows : (layer + 1) * rows].astype(out.dtype)


def in_vmem(kernel, out_shape, *operands, scratch=()):
    flops = 2 * operands[0].size * operands[1].shape[0]
    spec = pl.BlockSpec(memory_space=pltpu.VMEM)
    return pl.pallas_call(
        kernel,
        out_shape=out_shape,
        in_specs=[spec] * len(operands),
        out_specs=spec,
        scratch_shapes=scratch,
        compiler_params=pltpu.CompilerParams(vmem_limit_bytes=40 * 2**20),
        cost_estimate=pl.CostEstimate(flops=flops, bytes_accessed=2**20, transcendentals=0),
    )(*operands)


def on_device(groups, queries, fisher, train_grads):
    width, group = queries.shape[2], queries.shape[1]
    layers, slots = lax.axis_size("layer"), lax.axis_size("z")
    train = train_grads[0]
    cut = 4 * fisher.shape[2] * (slots * 7 // 16)

    mine = fisher[0].T
    fisher_got = lax.ppermute(mine, "xh", SWAP)
    early = lax.ppermute(train[:, :cut], "xh", SWAP)
    late = lax.ppermute(train[:, cut:], "xh", SWAP)

    wide = queries[0].astype(jnp.float32)
    exponent = exponent_of(jnp.max(jnp.abs(wide), axis=1, keepdims=True))
    scaled = (wide * jnp.exp2(TOP - exponent)).astype(jnp.float16)
    tail = jnp.broadcast_to(exponent, (group, 128)).astype(jnp.float16)
    rows = gather_z(jnp.concatenate([scaled, tail], axis=1), groups).reshape(slots * group, width + 128)
    rows, fisher_got = lax.optimization_barrier((rows, fisher_got))
    back = jnp.exp2(rows[:, width : width + 1].astype(jnp.float32) - TOP)
    rows = (rows[:, :width].astype(jnp.float32) * back).astype(jnp.bfloat16)
    rows_got = lax.ppermute(rows, "c", SWAP)

    height, span = slots * 2 * group, 2 * mine.shape[0]
    near = in_vmem(near_kernel, jax.ShapeDtypeStruct((height // 2, span), jnp.float32), rows, mine, fisher_got)
    chunk = in_vmem(
        chunk_kernel,
        jax.ShapeDtypeStruct((height + group, span), jnp.float32),
        near,
        rows_got,
        mine,
        fisher_got,
        scratch=[pltpu.VMEM((height, span), jnp.float32)],
    )
    chunk, early = lax.optimization_barrier((chunk, early))
    blocks = gather_z(chunk.astype(jnp.float16), groups)
    back = jnp.exp2(blocks[:, height : height + 1, :1].astype(jnp.float32) - TOP)
    own = (blocks[:, :height].astype(jnp.float32) * back).astype(jnp.bfloat16)
    other = lax.ppermute(own, "c", SWAP)
    parts_shape = jax.ShapeDtypeStruct((layers, 2, height // layers, train.shape[0]), jnp.float32)
    parts = in_vmem(score_kernel, parts_shape, own, other, train, early, late)

    parts = lax.all_to_all(parts.reshape(2 * layers, height // layers, -1), ("layer", "xh"), 0, 0)
    total = jnp.sum(parts.reshape(layers, 2, -1, 2 * group, parts.shape[-1]), axis=0)
    return jnp.swapaxes(total, 0, 1).reshape(-1, parts.shape[-1])


def solution(mesh):
    layers, spread = mesh.devices.shape
    slots = spread // 4
    fine = Mesh(mesh.devices.reshape(layers, slots, 2, 2), AXES)
    groups = [
        [layer * spread + 4 * z + 2 * chip + (side + z) % 2 for z in range(slots)]
        for layer in range(layers)
        for chip in range(2)
        for side in range(2)
    ]
    ex = ("z", "xh", "c")
    in_specs = (P("layer", ex, None), P("layer", None, ex), P("layer", ex, None))
    return jax.shard_map(
        functools.partial(on_device, groups),
        mesh=fine,
        in_specs=in_specs,
        out_specs=P("layer", ex),
        check_vma=False,
    )
```

```python
import functools

import jax
import jax.numpy as jnp
from jax import lax
from jax.experimental import pallas as pl
from jax.experimental.pallas import tpu as pltpu
from jax.sharding import Mesh, PartitionSpec as P

TOP = 14.0
AXES = ("layer", "z", "xh", "c")
SWAP = [(0, 1), (1, 0)]
NT = (((1,), (1,)), ((), ()))


def exponent_of(peak):
    return jnp.clip(jnp.floor(jnp.log2(jnp.maximum(peak, 1e-37))), -100.0, 100.0)


def gather_z(x, groups):
    return lax.all_gather(x, AXES, axis=0, axis_index_groups=groups)


def side_of():
    return lax.rem(lax.axis_index("c") + lax.axis_index("z"), 2)


def columns_of(mine, got):
    first = lax.axis_index("xh") == 0
    return jnp.concatenate([jnp.where(first, mine[...], got[...]), jnp.where(first, got[...], mine[...])], axis=0)


def rounded_product(rows, columns):
    value = lax.dot_general(rows[...], columns, NT, preferred_element_type=jnp.float32)
    return value.astype(jnp.bfloat16).astype(jnp.float32)


def near_kernel(rows, mine, got, out):
    out[...] = rounded_product(rows, columns_of(mine, got))


def chunk_kernel(near, rows, mine, got, out, order):
    side = side_of()
    far = rounded_product(rows, columns_of(mine, got))
    height = order.shape[0]
    group = out.shape[0] - height
    for z in range(height // (2 * group)):
        first = lax.rem(side + z, 2)
        piece = slice(z * group, (z + 1) * group)
        order[pl.ds(pl.multiple_of((2 * z + first) * group, group), group)] = near[piece]
        order[pl.ds(pl.multiple_of((2 * z + 1 - first) * group, group), group)] = far[piece]
    value = order[...]
    peak = jnp.max(jnp.max(jnp.abs(value), axis=0, keepdims=True), axis=1, keepdims=True)
    exponent = exponent_of(peak)
    tail = jnp.broadcast_to(exponent, (group, out.shape[1]))
    out[...] = jnp.concatenate([value * jnp.exp2(TOP - exponent), tail], axis=0)


def score_kernel(own, other, train, got, out):
    side, chip = side_of(), lax.axis_index("xh")
    layers, _, rows, count = out.shape
    half = own.shape[2] // 2
    here = jnp.zeros((own.shape[1], count), jnp.float32)
    there = here
    for z in range(own.shape[0]):
        mixed = lax.rem(side + z, 2) == 0
        one = jnp.where(mixed, own[z], other[z])
        two = jnp.where(mixed, other[z], own[z])
        left = jnp.concatenate([one[:, :half], two[:, :half], one[:, half:], two[:, half:]], axis=1)
        span = left.shape[1]
        right = train[:, z * span : (z + 1) * span]
        here = here + lax.dot_general(left, right, NT, preferred_element_type=jnp.float32)
        right = got[:, z * span : (z + 1) * span]
        there = there + lax.dot_general(left, right, NT, preferred_element_type=jnp.float32)
    for layer in range(layers):
        out[layer, chip] = here[layer * rows : (layer + 1) * rows].astype(out.dtype)
        out[layer, 1 - chip] = there[layer * rows : (layer + 1) * rows].astype(out.dtype)


def in_vmem(kernel, out_shape, *operands, scratch=()):
    flops = 2 * operands[0].size * operands[1].shape[0]
    spec = pl.BlockSpec(memory_space=pltpu.VMEM)
    return pl.pallas_call(
        kernel,
        out_shape=out_shape,
        in_specs=[spec] * len(operands),
        out_specs=spec,
        scratch_shapes=scratch,
        compiler_params=pltpu.CompilerParams(vmem_limit_bytes=40 * 2**20),
        cost_estimate=pl.CostEstimate(flops=flops, bytes_accessed=2**20, transcendentals=0),
    )(*operands)


def on_device(groups, queries, fisher, train_grads):
    width, group = queries.shape[2], queries.shape[1]
    layers, slots = lax.axis_size("layer"), lax.axis_size("z")
    train = train_grads[0]

    mine = fisher[0].T
    fisher_got = lax.ppermute(mine, "xh", SWAP)
    train_got = lax.ppermute(train, "xh", SWAP)

    wide = queries[0].astype(jnp.float32)
    exponent = exponent_of(jnp.max(jnp.abs(wide), axis=1, keepdims=True))
    scaled = (wide * jnp.exp2(TOP - exponent)).astype(jnp.float16)
    tail = jnp.broadcast_to(exponent, (group, 128)).astype(jnp.float16)
    rows = gather_z(jnp.concatenate([scaled, tail], axis=1), groups).reshape(slots * group, width + 128)
    rows, fisher_got = lax.optimization_barrier((rows, fisher_got))
    back = jnp.exp2(rows[:, width : width + 1].astype(jnp.float32) - TOP)
    rows = (rows[:, :width].astype(jnp.float32) * back).astype(jnp.bfloat16)
    rows_got = lax.ppermute(rows, "c", SWAP)

    height, span = slots * 2 * group, 2 * mine.shape[0]
    near = in_vmem(near_kernel, jax.ShapeDtypeStruct((height // 2, span), jnp.float32), rows, mine, fisher_got)
    chunk = in_vmem(
        chunk_kernel,
        jax.ShapeDtypeStruct((height + group, span), jnp.float32),
        near,
        rows_got,
        mine,
        fisher_got,
        scratch=[pltpu.VMEM((height, span), jnp.float32)],
    )
    blocks = gather_z(chunk.astype(jnp.float16), groups)
    back = jnp.exp2(blocks[:, height : height + 1, :1].astype(jnp.float32) - TOP)
    own = (blocks[:, :height].astype(jnp.float32) * back).astype(jnp.bfloat16)
    other = lax.ppermute(own, "c", SWAP)
    parts_shape = jax.ShapeDtypeStruct((layers, 2, height // layers, train.shape[0]), jnp.float32)
    parts = in_vmem(score_kernel, parts_shape, own, other, train, train_got)

    parts = lax.all_to_all(parts.reshape(2 * layers, height // layers, -1), ("layer", "xh"), 0, 0)
    total = jnp.sum(parts.reshape(layers, 2, -1, 2 * group, parts.shape[-1]), axis=0)
    return jnp.swapaxes(total, 0, 1).reshape(-1, parts.shape[-1])


def solution(mesh):
    layers, spread = mesh.devices.shape
    slots = spread // 4
    fine = Mesh(mesh.devices.reshape(layers, slots, 2, 2), AXES)
    groups = [
        [layer * spread + 4 * z + 2 * chip + (side + z) % 2 for z in range(slots)]
        for layer in range(layers)
        for chip in range(2)
        for side in range(2)
    ]
    ex = ("z", "xh", "c")
    in_specs = (P("layer", ex, None), P("layer", None, ex), P("layer", ex, None))
    return jax.shard_map(
        functools.partial(on_device, groups),
        mesh=fine,
        in_specs=in_specs,
        out_specs=P("layer", ex),
        check_vma=False,
    )
```

```python
import functools

import jax
import jax.numpy as jnp
from jax import lax
from jax.experimental import pallas as pl
from jax.experimental.pallas import tpu as pltpu
from jax.sharding import Mesh, PartitionSpec as P

TOP = 14.0
AXES = ("layer", "z", "xh", "c")
SWAP = [(0, 1), (1, 0)]
NT = (((1,), (1,)), ((), ()))


def exponent_of(peak):
    return jnp.clip(jnp.floor(jnp.log2(jnp.maximum(peak, 1e-37))), -100.0, 100.0)


def gather_z(x, groups):
    return lax.all_gather(x, AXES, axis=0, axis_index_groups=groups)


def side_of():
    return lax.rem(lax.axis_index("c") + lax.axis_index("z"), 2)


def columns_of(mine, got):
    first = lax.axis_index("xh") == 0
    return jnp.concatenate([jnp.where(first, mine[...], got[...]), jnp.where(first, got[...], mine[...])], axis=0)


def rounded_product(rows, columns):
    value = lax.dot_general(rows[...], columns, NT, preferred_element_type=jnp.float32)
    return value.astype(jnp.bfloat16).astype(jnp.float32)


def near_kernel(rows, mine, got, out):
    out[...] = rounded_product(rows, columns_of(mine, got))


def chunk_kernel(near, rows, mine, got, out, order):
    side = side_of()
    far = rounded_product(rows, columns_of(mine, got))
    height = order.shape[0]
    group = out.shape[0] - height
    for z in range(height // (2 * group)):
        first = lax.rem(side + z, 2)
        piece = slice(z * group, (z + 1) * group)
        order[pl.ds(pl.multiple_of((2 * z + first) * group, group), group)] = near[piece]
        order[pl.ds(pl.multiple_of((2 * z + 1 - first) * group, group), group)] = far[piece]
    value = order[...]
    peak = jnp.max(jnp.max(jnp.abs(value), axis=0, keepdims=True), axis=1, keepdims=True)
    exponent = exponent_of(peak)
    tail = jnp.broadcast_to(exponent, (group, out.shape[1]))
    out[...] = jnp.concatenate([value * jnp.exp2(TOP - exponent), tail], axis=0)


def score_kernel(own, other, train, got, out):
    side, chip = side_of(), lax.axis_index("xh")
    layers, _, rows, count = out.shape
    half = own.shape[2] // 2
    here = jnp.zeros((own.shape[1], count), jnp.float32)
    there = here
    for z in range(own.shape[0]):
        mixed = lax.rem(side + z, 2) == 0
        one = jnp.where(mixed, own[z], other[z])
        two = jnp.where(mixed, other[z], own[z])
        left = jnp.concatenate([one[:, :half], two[:, :half], one[:, half:], two[:, half:]], axis=1)
        span = left.shape[1]
        right = train[:, z * span : (z + 1) * span]
        here = here + lax.dot_general(left, right, NT, preferred_element_type=jnp.float32)
        right = got[:, z * span : (z + 1) * span]
        there = there + lax.dot_general(left, right, NT, preferred_element_type=jnp.float32)
    for layer in range(layers):
        out[layer, chip] = here[layer * rows : (layer + 1) * rows].astype(out.dtype)
        out[layer, 1 - chip] = there[layer * rows : (layer + 1) * rows].astype(out.dtype)


def in_vmem(kernel, out_shape, *operands, scratch=()):
    flops = 2 * operands[0].size * operands[1].shape[0]
    spec = pl.BlockSpec(memory_space=pltpu.VMEM)
    return pl.pallas_call(
        kernel,
        out_shape=out_shape,
        in_specs=[spec] * len(operands),
        out_specs=spec,
        scratch_shapes=scratch,
        compiler_params=pltpu.CompilerParams(vmem_limit_bytes=40 * 2**20),
        cost_estimate=pl.CostEstimate(flops=flops, bytes_accessed=2**20, transcendentals=0),
    )(*operands)


def on_device(groups, queries, fisher, train_grads):
    width, group = queries.shape[2], queries.shape[1]
    layers, slots = lax.axis_size("layer"), lax.axis_size("z")
    train = train_grads[0]

    mine = fisher[0].T
    fisher_got = lax.ppermute(mine, "xh", SWAP)
    train_got = lax.ppermute(train, "xh", SWAP)

    wide = queries[0].astype(jnp.float32)
    exponent = exponent_of(jnp.max(jnp.abs(wide), axis=1, keepdims=True))
    scaled = (wide * jnp.exp2(TOP - exponent)).astype(jnp.float16)
    tail = jnp.broadcast_to(exponent, (group, 128)).astype(jnp.float16)
    rows = gather_z(jnp.concatenate([scaled, tail], axis=1), groups).reshape(slots * group, width + 128)
    rows, fisher_got = lax.optimization_barrier((rows, fisher_got))
    back = jnp.exp2(rows[:, width : width + 1].astype(jnp.float32) - TOP)
    rows = (rows[:, :width].astype(jnp.float32) * back).astype(jnp.bfloat16)
    rows_got = lax.ppermute(rows, "c", SWAP)

    height, span = slots * 2 * group, 2 * mine.shape[0]
    near = in_vmem(near_kernel, jax.ShapeDtypeStruct((height // 2, span), jnp.float32), rows, mine, fisher_got)
    chunk = in_vmem(
        chunk_kernel,
        jax.ShapeDtypeStruct((height + group, span), jnp.float32),
        near,
        rows_got,
        mine,
        fisher_got,
        scratch=[pltpu.VMEM((height, span), jnp.float32)],
    )
    blocks = gather_z(chunk.astype(jnp.float16), groups)
    back = jnp.exp2(blocks[:, height : height + 1, :1].astype(jnp.float32) - TOP)
    own = (blocks[:, :height].astype(jnp.float32) * back).astype(jnp.bfloat16)
    other = lax.ppermute(own, "c", SWAP)
    parts_shape = jax.ShapeDtypeStruct((layers, 2, height // layers, train.shape[0]), jnp.bfloat16)
    parts = in_vmem(score_kernel, parts_shape, own, other, train, train_got)

    parts = lax.all_to_all(parts.reshape(2 * layers, height // layers, -1), ("layer", "xh"), 0, 0)
    parts = parts.reshape(layers, 2, -1, 2 * group, parts.shape[-1])
    total = jnp.sum(parts.astype(jnp.float32), axis=0)
    return jnp.swapaxes(total, 0, 1).reshape(-1, parts.shape[-1])


def solution(mesh):
    layers, spread = mesh.devices.shape
    slots = spread // 4
    fine = Mesh(mesh.devices.reshape(layers, slots, 2, 2), AXES)
    groups = [
        [layer * spread + 4 * z + 2 * chip + (side + z) % 2 for z in range(slots)]
        for layer in range(layers)
        for chip in range(2)
        for side in range(2)
    ]
    ex = ("z", "xh", "c")
    in_specs = (P("layer", ex, None), P("layer", None, ex), P("layer", ex, None))
    return jax.shard_map(
        functools.partial(on_device, groups),
        mesh=fine,
        in_specs=in_specs,
        out_specs=P("layer", ex),
        check_vma=False,
    )
```

```python
import functools

import jax
import jax.numpy as jnp
from jax import lax
from jax.experimental import pallas as pl
from jax.experimental.pallas import tpu as pltpu
from jax.sharding import Mesh, PartitionSpec as P

TOP = 14.0
AXES = ("layer", "z", "xh", "c")
SWAP = [(0, 1), (1, 0)]
NT = (((1,), (1,)), ((), ()))


def exponent_of(peak):
    return jnp.clip(jnp.floor(jnp.log2(jnp.maximum(peak, 1e-37))), -100.0, 100.0)


def gather_z(x, groups):
    return lax.all_gather(x, AXES, axis=0, axis_index_groups=groups)


def side_of():
    return lax.rem(lax.axis_index("c") + lax.axis_index("z"), 2)


def columns_of(mine, got):
    first = lax.axis_index("xh") == 0
    return jnp.concatenate([jnp.where(first, mine[...], got[...]), jnp.where(first, got[...], mine[...])], axis=0)


def rounded_product(rows, columns):
    value = lax.dot_general(rows[...], columns, NT, preferred_element_type=jnp.float32)
    return value.astype(jnp.bfloat16).astype(jnp.float32)


def scale_kernel(rows, out):
    value = rows[...].astype(jnp.float32)
    exponent = exponent_of(jnp.max(jnp.abs(value), axis=1, keepdims=True))
    out[:, : value.shape[1]] = value * jnp.exp2(TOP - exponent)
    out[:, value.shape[1] :] = jnp.broadcast_to(exponent, (value.shape[0], 128))


def sum_kernel(parts, out):
    span = out.shape[0] // 4
    for z in range(2):
        for chip in range(2):
            piece = parts[chip, z * span : (z + 1) * span].astype(jnp.float32)
            for layer in range(1, parts.shape[0] // 2):
                piece = piece + parts[2 * layer + chip, z * span : (z + 1) * span].astype(jnp.float32)
            begin = (2 * z + chip) * span
            out[begin : begin + span] = piece


def near_kernel(rows, mine, got, out):
    out[...] = rounded_product(rows, columns_of(mine, got))


def chunk_kernel(near, rows, mine, got, out, order):
    side = side_of()
    far = rounded_product(rows, columns_of(mine, got))
    height = order.shape[0]
    group = out.shape[0] - height
    for z in range(height // (2 * group)):
        first = lax.rem(side + z, 2)
        piece = slice(z * group, (z + 1) * group)
        order[pl.ds(pl.multiple_of((2 * z + first) * group, group), group)] = near[piece]
        order[pl.ds(pl.multiple_of((2 * z + 1 - first) * group, group), group)] = far[piece]
    value = order[...]
    peak = jnp.max(jnp.max(jnp.abs(value), axis=0, keepdims=True), axis=1, keepdims=True)
    exponent = exponent_of(peak)
    tail = jnp.broadcast_to(exponent, (group, out.shape[1]))
    out[...] = jnp.concatenate([value * jnp.exp2(TOP - exponent), tail], axis=0)


def score_kernel(own, other, train, got, out):
    side, chip = side_of(), lax.axis_index("xh")
    layers, _, rows, count = out.shape
    half = own.shape[2] // 2
    here = jnp.zeros((own.shape[1], count), jnp.float32)
    there = here
    for z in range(own.shape[0]):
        mixed = lax.rem(side + z, 2) == 0
        one = jnp.where(mixed, own[z], other[z])
        two = jnp.where(mixed, other[z], own[z])
        left = jnp.concatenate([one[:, :half], two[:, :half], one[:, half:], two[:, half:]], axis=1)
        span = left.shape[1]
        right = train[:, z * span : (z + 1) * span]
        here = here + lax.dot_general(left, right, NT, preferred_element_type=jnp.float32)
        right = got[:, z * span : (z + 1) * span]
        there = there + lax.dot_general(left, right, NT, preferred_element_type=jnp.float32)
    for layer in range(layers):
        out[layer, chip] = here[layer * rows : (layer + 1) * rows].astype(out.dtype)
        out[layer, 1 - chip] = there[layer * rows : (layer + 1) * rows].astype(out.dtype)


def in_vmem(kernel, out_shape, *operands, scratch=()):
    flops = 2 * operands[0].size * operands[-1].shape[0]
    spec = pl.BlockSpec(memory_space=pltpu.VMEM)
    return pl.pallas_call(
        kernel,
        out_shape=out_shape,
        in_specs=[spec] * len(operands),
        out_specs=spec,
        scratch_shapes=scratch,
        compiler_params=pltpu.CompilerParams(vmem_limit_bytes=40 * 2**20),
        cost_estimate=pl.CostEstimate(flops=flops, bytes_accessed=2**20, transcendentals=0),
    )(*operands)


def on_device(groups, queries, fisher, train_grads):
    width, group = queries.shape[2], queries.shape[1]
    layers, slots = lax.axis_size("layer"), lax.axis_size("z")
    train = train_grads[0]

    mine = fisher[0].T
    fisher_got = lax.ppermute(mine, "xh", SWAP)
    train_got = lax.ppermute(train, "xh", SWAP)

    scaled = in_vmem(scale_kernel, jax.ShapeDtypeStruct((group, width + 128), jnp.float32), queries[0])
    rows = gather_z(scaled.astype(jnp.float16), groups).reshape(slots * group, width + 128)
    rows, fisher_got = lax.optimization_barrier((rows, fisher_got))
    back = jnp.exp2(rows[:, width : width + 1].astype(jnp.float32) - TOP)
    rows = (rows[:, :width].astype(jnp.float32) * back).astype(jnp.bfloat16)
    rows_got = lax.ppermute(rows, "c", SWAP)

    height, span = slots * 2 * group, 2 * mine.shape[0]
    near = in_vmem(near_kernel, jax.ShapeDtypeStruct((height // 2, span), jnp.float32), rows, mine, fisher_got)
    chunk = in_vmem(
        chunk_kernel,
        jax.ShapeDtypeStruct((height + group, span), jnp.float32),
        near,
        rows_got,
        mine,
        fisher_got,
        scratch=[pltpu.VMEM((height, span), jnp.float32)],
    )
    blocks = gather_z(chunk.astype(jnp.float16), groups)
    back = jnp.exp2(blocks[:, height : height + 1, :1].astype(jnp.float32) - TOP)
    own = (blocks[:, :height].astype(jnp.float32) * back).astype(jnp.bfloat16)
    other = lax.ppermute(own, "c", SWAP)
    parts_shape = jax.ShapeDtypeStruct((layers, 2, height // layers, train.shape[0]), jnp.bfloat16)
    parts = in_vmem(score_kernel, parts_shape, own, other, train, train_got)

    parts = lax.all_to_all(parts.reshape(2 * layers, height // layers, -1), ("layer", "xh"), 0, 0)
    return in_vmem(sum_kernel, jax.ShapeDtypeStruct((2 * height // layers, parts.shape[2]), jnp.float32), parts)


def solution(mesh):
    layers, spread = mesh.devices.shape
    slots = spread // 4
    fine = Mesh(mesh.devices.reshape(layers, slots, 2, 2), AXES)
    groups = [
        [layer * spread + 4 * z + 2 * chip + (side + z) % 2 for z in range(slots)]
        for layer in range(layers)
        for chip in range(2)
        for side in range(2)
    ]
    ex = ("z", "xh", "c")
    in_specs = (P("layer", ex, None), P("layer", None, ex), P("layer", ex, None))
    return jax.shard_map(
        functools.partial(on_device, groups),
        mesh=fine,
        in_specs=in_specs,
        out_specs=P("layer", ex),
        check_vma=False,
    )
```

```python
import functools

import jax
import jax.numpy as jnp
from jax import lax
from jax.experimental import pallas as pl
from jax.experimental.pallas import tpu as pltpu
from jax.sharding import Mesh, PartitionSpec as P

TOP = 14.0
AXES = ("layer", "z", "xh", "c")
SWAP = [(0, 1), (1, 0)]
NT = (((1,), (1,)), ((), ()))


def exponent_of(peak):
    return jnp.clip(jnp.floor(jnp.log2(jnp.maximum(peak, 1e-37))), -100.0, 100.0)


def gather_z(x, groups):
    return lax.all_gather(x, AXES, axis=0, axis_index_groups=groups)


def side_of():
    return lax.rem(lax.axis_index("c") + lax.axis_index("z"), 2)


def columns_of(mine, got):
    first = lax.axis_index("xh") == 0
    return jnp.concatenate([jnp.where(first, mine[...], got[...]), jnp.where(first, got[...], mine[...])], axis=0)


def rounded_product(rows, columns):
    value = lax.dot_general(rows[...], columns, NT, preferred_element_type=jnp.float32)
    return value.astype(jnp.bfloat16).astype(jnp.float32)


def scale_kernel(rows, out):
    value = rows[...].astype(jnp.float32)
    exponent = exponent_of(jnp.max(jnp.abs(value), axis=1, keepdims=True))
    out[:, : value.shape[1]] = value * jnp.exp2(TOP - exponent)
    out[:, value.shape[1] :] = jnp.broadcast_to(exponent, (value.shape[0], 128))


def sum_kernel(parts, out):
    span = out.shape[0] // 4
    for z in range(2):
        for chip in range(2):
            piece = parts[chip, z * span : (z + 1) * span].astype(jnp.float32)
            for layer in range(1, parts.shape[0] // 2):
                piece = piece + parts[2 * layer + chip, z * span : (z + 1) * span].astype(jnp.float32)
            begin = (2 * z + chip) * span
            out[begin : begin + span] = piece


def near_kernel(rows, mine, got, out):
    out[...] = rounded_product(rows, columns_of(mine, got))


def chunk_kernel(near, rows, mine, got, out, order):
    side = side_of()
    far = rounded_product(rows, columns_of(mine, got))
    height = order.shape[0]
    group = out.shape[0] - height
    for z in range(height // (2 * group)):
        first = lax.rem(side + z, 2)
        piece = slice(z * group, (z + 1) * group)
        order[pl.ds(pl.multiple_of((2 * z + first) * group, group), group)] = near[piece]
        order[pl.ds(pl.multiple_of((2 * z + 1 - first) * group, group), group)] = far[piece]
    value = order[...]
    peak = jnp.max(jnp.max(jnp.abs(value), axis=0, keepdims=True), axis=1, keepdims=True)
    exponent = exponent_of(peak)
    tail = jnp.broadcast_to(exponent, (group, out.shape[1]))
    out[...] = jnp.concatenate([value * jnp.exp2(TOP - exponent), tail], axis=0)


def scores(own, other, train):
    side = side_of()
    half = own.shape[2] // 2
    total = jnp.zeros((own.shape[1], train.shape[0]), jnp.float32)
    for z in range(own.shape[0]):
        mixed = lax.rem(side + z, 2) == 0
        one = jnp.where(mixed, own[z], other[z])
        two = jnp.where(mixed, other[z], own[z])
        left = jnp.concatenate([one[:, :half], two[:, :half], one[:, half:], two[:, half:]], axis=1)
        right = train[:, z * left.shape[1] : (z + 1) * left.shape[1]]
        total = total + lax.dot_general(left, right, NT, preferred_element_type=jnp.float32)
    return total


def here_kernel(own, other, train, out):
    out[...] = scores(own, other, train).astype(out.dtype)


def there_kernel(own, other, here, train, out):
    chip = lax.axis_index("xh")
    layers, _, rows, _ = out.shape
    there = scores(own, other, train).astype(out.dtype)
    for layer in range(layers):
        piece = slice(layer * rows, (layer + 1) * rows)
        out[layer, chip] = here[piece]
        out[layer, 1 - chip] = there[piece]


def in_vmem(kernel, out_shape, *operands, scratch=()):
    flops = 2 * operands[0].size * operands[-1].shape[0]
    spec = pl.BlockSpec(memory_space=pltpu.VMEM)
    return pl.pallas_call(
        kernel,
        out_shape=out_shape,
        in_specs=[spec] * len(operands),
        out_specs=spec,
        scratch_shapes=scratch,
        compiler_params=pltpu.CompilerParams(vmem_limit_bytes=40 * 2**20),
        cost_estimate=pl.CostEstimate(flops=flops, bytes_accessed=2**20, transcendentals=0),
    )(*operands)


def on_device(groups, queries, fisher, train_grads):
    width, group = queries.shape[2], queries.shape[1]
    layers, slots = lax.axis_size("layer"), lax.axis_size("z")
    train = train_grads[0]

    mine = fisher[0].T
    fisher_got = lax.ppermute(mine, "xh", SWAP)
    train_got = lax.ppermute(train, "xh", SWAP)

    scaled = in_vmem(scale_kernel, jax.ShapeDtypeStruct((group, width + 128), jnp.float32), queries[0])
    rows = gather_z(scaled.astype(jnp.float16), groups).reshape(slots * group, width + 128)
    rows, fisher_got = lax.optimization_barrier((rows, fisher_got))
    back = jnp.exp2(rows[:, width : width + 1].astype(jnp.float32) - TOP)
    rows = (rows[:, :width].astype(jnp.float32) * back).astype(jnp.bfloat16)
    rows_got = lax.ppermute(rows, "c", SWAP)

    height, span = slots * 2 * group, 2 * mine.shape[0]
    near = in_vmem(near_kernel, jax.ShapeDtypeStruct((height // 2, span), jnp.float32), rows, mine, fisher_got)
    chunk = in_vmem(
        chunk_kernel,
        jax.ShapeDtypeStruct((height + group, span), jnp.float32),
        near,
        rows_got,
        mine,
        fisher_got,
        scratch=[pltpu.VMEM((height, span), jnp.float32)],
    )
    blocks = gather_z(chunk.astype(jnp.float16), groups)
    back = jnp.exp2(blocks[:, height : height + 1, :1].astype(jnp.float32) - TOP)
    own = (blocks[:, :height].astype(jnp.float32) * back).astype(jnp.bfloat16)
    other = lax.ppermute(own, "c", SWAP)
    here = in_vmem(here_kernel, jax.ShapeDtypeStruct((height, train.shape[0]), jnp.bfloat16), own, other, train)
    parts_shape = jax.ShapeDtypeStruct((layers, 2, height // layers, train.shape[0]), jnp.bfloat16)
    parts = in_vmem(there_kernel, parts_shape, own, other, here, train_got)

    parts = lax.all_to_all(parts.reshape(2 * layers, height // layers, -1), ("layer", "xh"), 0, 0)
    return in_vmem(sum_kernel, jax.ShapeDtypeStruct((2 * height // layers, parts.shape[2]), jnp.float32), parts)


def solution(mesh):
    layers, spread = mesh.devices.shape
    slots = spread // 4
    fine = Mesh(mesh.devices.reshape(layers, slots, 2, 2), AXES)
    groups = [
        [layer * spread + 4 * z + 2 * chip + (side + z) % 2 for z in range(slots)]
        for layer in range(layers)
        for chip in range(2)
        for side in range(2)
    ]
    ex = ("z", "xh", "c")
    in_specs = (P("layer", ex, None), P("layer", None, ex), P("layer", ex, None))
    return jax.shard_map(
        functools.partial(on_device, groups),
        mesh=fine,
        in_specs=in_specs,
        out_specs=P("layer", ex),
        check_vma=False,
    )
```

```python
import functools

import jax
import jax.numpy as jnp
from jax import lax
from jax.experimental import pallas as pl
from jax.experimental.pallas import tpu as pltpu
from jax.sharding import Mesh, PartitionSpec as P

TOP = 14.0
AXES = ("layer", "z", "xh", "c")
SWAP = [(0, 1), (1, 0)]
NT = (((1,), (1,)), ((), ()))


def exponent_of(peak):
    return jnp.clip(jnp.floor(jnp.log2(jnp.maximum(peak, 1e-37))), -100.0, 100.0)


def gather_z(x, groups):
    return lax.all_gather(x, AXES, axis=0, axis_index_groups=groups)


def core_at(entry, z):
    return lax.rem(entry + lax.axis_index("z") + z, 2)


def columns_of(mine, got):
    first = lax.axis_index("xh") == 0
    return jnp.concatenate([jnp.where(first, mine[...], got[...]), jnp.where(first, got[...], mine[...])], axis=0)


def rounded_product(rows, columns):
    value = lax.dot_general(rows[...], columns, NT, preferred_element_type=jnp.float32)
    return value.astype(jnp.bfloat16).astype(jnp.float32)


def scale_kernel(rows, out):
    value = rows[...].astype(jnp.float32)
    exponent = exponent_of(jnp.max(jnp.abs(value), axis=1, keepdims=True))
    out[:, : value.shape[1]] = value * jnp.exp2(TOP - exponent)
    out[:, value.shape[1] :] = jnp.broadcast_to(exponent, (value.shape[0], 128))


def sum_kernel(parts, out):
    span = out.shape[0] // 4
    for z in range(2):
        for chip in range(2):
            piece = parts[chip, z * span : (z + 1) * span].astype(jnp.float32)
            for layer in range(1, parts.shape[0] // 2):
                piece = piece + parts[2 * layer + chip, z * span : (z + 1) * span].astype(jnp.float32)
            begin = (2 * z + chip) * span
            out[begin : begin + span] = piece


def scale_kernel(rows, out):
    value = rows[...].astype(jnp.float32)
    exponent = exponent_of(jnp.max(jnp.abs(value), axis=1, keepdims=True))
    out[:, : value.shape[1]] = value * jnp.exp2(TOP - exponent)
    out[:, value.shape[1] :] = jnp.broadcast_to(exponent, (value.shape[0], 128))


def sum_kernel(parts, out):
    span = out.shape[0] // 4
    for z in range(2):
        for chip in range(2):
            piece = parts[chip, z * span : (z + 1) * span].astype(jnp.float32)
            for layer in range(1, parts.shape[0] // 2):
                piece = piece + parts[2 * layer + chip, z * span : (z + 1) * span].astype(jnp.float32)
            begin = (2 * z + chip) * span
            out[begin : begin + span] = piece


def near_kernel(rows, mine, got, out):
    out[...] = rounded_product(rows, columns_of(mine, got))


def chunk_kernel(rows, mine, got, out, order):
    product = rounded_product(rows, columns_of(mine, got))
    height = order.shape[0]
    group = out.shape[0] - height
    slots = height // (2 * group)
    for entry in range(2):
        for z in range(slots):
            begin = (entry * slots + z) * group
            place = pl.multiple_of((2 * z + core_at(entry, z)) * group, group)
            order[pl.ds(place, group)] = product[begin : begin + group]
    value = order[...]
    peak = jnp.max(jnp.max(jnp.abs(value), axis=0, keepdims=True), axis=1, keepdims=True)
    exponent = exponent_of(peak)
    tail = jnp.broadcast_to(exponent, (group, out.shape[1]))
    out[...] = jnp.concatenate([value * jnp.exp2(TOP - exponent), tail], axis=0)


def scores(blocks, train):
    half = blocks.shape[3] // 2
    total = jnp.zeros((blocks.shape[2], train.shape[0]), jnp.float32)
    for z in range(blocks.shape[1]):
        straight = core_at(0, z) == 0
        one = jnp.where(straight, blocks[0, z], blocks[1, z])
        two = jnp.where(straight, blocks[1, z], blocks[0, z])
        left = jnp.concatenate([one[:, :half], two[:, :half], one[:, half:], two[:, half:]], axis=1)
        right = train[:, z * left.shape[1] : (z + 1) * left.shape[1]]
        total = total + lax.dot_general(left, right, NT, preferred_element_type=jnp.float32)
    return total


def here_kernel(blocks, train, out):
    out[...] = scores(blocks, train).astype(out.dtype)


def there_kernel(blocks, here, train, out):
    chip = lax.axis_index("xh")
    layers, _, rows, _ = out.shape
    there = scores(blocks, train).astype(out.dtype)
    for layer in range(layers):
        piece = slice(layer * rows, (layer + 1) * rows)
        out[layer, chip] = here[piece]
        out[layer, 1 - chip] = there[piece]


def in_vmem(kernel, out_shape, *operands, scratch=()):
    flops = 2 * operands[0].size * operands[-1].shape[0]
    spec = pl.BlockSpec(memory_space=pltpu.VMEM)
    return pl.pallas_call(
        kernel,
        out_shape=out_shape,
        in_specs=[spec] * len(operands),
        out_specs=spec,
        scratch_shapes=scratch,
        compiler_params=pltpu.CompilerParams(vmem_limit_bytes=40 * 2**20),
        cost_estimate=pl.CostEstimate(flops=flops, bytes_accessed=2**20, transcendentals=0),
    )(*operands)


def on_device(groups, queries, fisher, train_grads):
    width, group = queries.shape[2], queries.shape[1]
    layers, slots = lax.axis_size("layer"), lax.axis_size("z")
    train = train_grads[0]

    mine = fisher[0].T
    fisher_got = lax.ppermute(mine, "xh", SWAP)
    train_got = lax.ppermute(train, "xh", SWAP)

    scaled = in_vmem(scale_kernel, jax.ShapeDtypeStruct((group, width + 128), jnp.float32), queries[0])
    rows = gather_z(scaled.astype(jnp.float16), groups).reshape(slots * group, width + 128)
    rows = lax.all_gather(rows, "c", axis=0, tiled=True)
    rows, fisher_got = lax.optimization_barrier((rows, fisher_got))
    back = jnp.exp2(rows[:, width : width + 1].astype(jnp.float32) - TOP)
    rows = (rows[:, :width].astype(jnp.float32) * back).astype(jnp.bfloat16)

    height, span = slots * 2 * group, 2 * mine.shape[0]
    chunk = in_vmem(
        chunk_kernel,
        jax.ShapeDtypeStruct((height + group, span), jnp.float32),
        rows,
        mine,
        fisher_got,
        scratch=[pltpu.VMEM((height, span), jnp.float32)],
    )
    blocks = lax.all_gather(gather_z(chunk.astype(jnp.float16), groups), "c", axis=0)
    back = jnp.exp2(blocks[:, :, height : height + 1, :1].astype(jnp.float32) - TOP)
    blocks = (blocks[:, :, :height].astype(jnp.float32) * back).astype(jnp.bfloat16)
    here = in_vmem(here_kernel, jax.ShapeDtypeStruct((height, train.shape[0]), jnp.bfloat16), blocks, train)
    parts_shape = jax.ShapeDtypeStruct((layers, 2, height // layers, train.shape[0]), jnp.bfloat16)
    parts = in_vmem(there_kernel, parts_shape, blocks, here, train_got)

    parts = lax.all_to_all(parts.reshape(2 * layers, height // layers, -1), ("layer", "xh"), 0, 0)
    return in_vmem(sum_kernel, jax.ShapeDtypeStruct((2 * height // layers, parts.shape[2]), jnp.float32), parts)


def solution(mesh):
    layers, spread = mesh.devices.shape
    slots = spread // 4
    fine = Mesh(mesh.devices.reshape(layers, slots, 2, 2), AXES)
    groups = [
        [layer * spread + 4 * z + 2 * chip + (side + z) % 2 for z in range(slots)]
        for layer in range(layers)
        for chip in range(2)
        for side in range(2)
    ]
    ex = ("z", "xh", "c")
    in_specs = (P("layer", ex, None), P("layer", None, ex), P("layer", ex, None))
    return jax.shard_map(
        functools.partial(on_device, groups),
        mesh=fine,
        in_specs=in_specs,
        out_specs=P("layer", ex),
        check_vma=False,
    )
```

```python
import functools

import jax
import jax.numpy as jnp
from jax import lax
from jax.experimental import pallas as pl
from jax.experimental.pallas import tpu as pltpu
from jax.sharding import Mesh, PartitionSpec as P

TOP = 14.0
AXES = ("layer", "z", "xh", "c")
SWAP = [(0, 1), (1, 0)]
NT = (((1,), (1,)), ((), ()))


def exponent_of(peak):
    return jnp.clip(jnp.floor(jnp.log2(jnp.maximum(peak, 1e-37))), -100.0, 100.0)


def gather_z(x, groups):
    return lax.all_gather(x, AXES, axis=0, axis_index_groups=groups)


def core_at(entry, z):
    return lax.rem(entry + lax.axis_index("z") + z, 2)


def columns_of(mine, got):
    first = lax.axis_index("xh") == 0
    return jnp.concatenate([jnp.where(first, mine[...], got[...]), jnp.where(first, got[...], mine[...])], axis=0)


def rounded_product(rows, columns):
    value = lax.dot_general(rows[...], columns, NT, preferred_element_type=jnp.float32)
    return value.astype(jnp.bfloat16).astype(jnp.float32)


def scale_kernel(rows, out):
    value = rows[...].astype(jnp.float32)
    exponent = exponent_of(jnp.max(jnp.abs(value), axis=1, keepdims=True))
    out[:, : value.shape[1]] = value * jnp.exp2(TOP - exponent)
    out[:, value.shape[1] :] = jnp.broadcast_to(exponent, (value.shape[0], 128))


def sum_kernel(parts, out):
    span = out.shape[0] // 4
    for z in range(2):
        for chip in range(2):
            piece = parts[chip, z * span : (z + 1) * span].astype(jnp.float32)
            for layer in range(1, parts.shape[0] // 2):
                piece = piece + parts[2 * layer + chip, z * span : (z + 1) * span].astype(jnp.float32)
            begin = (2 * z + chip) * span
            out[begin : begin + span] = piece


def scale_kernel(rows, out):
    value = rows[...].astype(jnp.float32)
    exponent = exponent_of(jnp.max(jnp.abs(value), axis=1, keepdims=True))
    out[:, : value.shape[1]] = value * jnp.exp2(TOP - exponent)
    out[:, value.shape[1] :] = jnp.broadcast_to(exponent, (value.shape[0], 128))


def sum_kernel(parts, out):
    span = out.shape[0] // 4
    for z in range(2):
        for chip in range(2):
            piece = parts[chip, z * span : (z + 1) * span].astype(jnp.float32)
            for layer in range(1, parts.shape[0] // 2):
                piece = piece + parts[2 * layer + chip, z * span : (z + 1) * span].astype(jnp.float32)
            begin = (2 * z + chip) * span
            out[begin : begin + span] = piece


def near_kernel(rows, mine, got, out):
    out[...] = rounded_product(rows, columns_of(mine, got))


def chunk_kernel(rows, mine, got, out, order):
    product = rounded_product(rows, columns_of(mine, got))
    height = order.shape[0]
    group = out.shape[0] - height
    slots = height // (2 * group)
    for entry in range(2):
        for z in range(slots):
            begin = (entry * slots + z) * group
            place = pl.multiple_of((2 * z + core_at(entry, z)) * group, group)
            order[pl.ds(place, group)] = product[begin : begin + group]
    value = order[...]
    peak = jnp.max(jnp.max(jnp.abs(value), axis=0, keepdims=True), axis=1, keepdims=True)
    exponent = exponent_of(peak)
    tail = jnp.broadcast_to(exponent, (group, out.shape[1]))
    out[...] = jnp.concatenate([value * jnp.exp2(TOP - exponent), tail], axis=0)


def scores(blocks, train, arrive=lambda z: None):
    half = blocks.shape[3] // 2
    total = jnp.zeros((blocks.shape[2], train.shape[0]), jnp.float32)
    for z in range(blocks.shape[1]):
        arrive(z)
        straight = core_at(0, z) == 0
        one = jnp.where(straight, blocks[0, z], blocks[1, z])
        two = jnp.where(straight, blocks[1, z], blocks[0, z])
        left = jnp.concatenate([one[:, :half], two[:, :half], one[:, half:], two[:, half:]], axis=1)
        right = train[:, z * left.shape[1] : (z + 1) * left.shape[1]]
        total = total + lax.dot_general(left, right, NT, preferred_element_type=jnp.float32)
    return total


def here_kernel(blocks, train, out, held, done):
    count = done.shape[0]
    span = train.shape[1] // count
    copies = []
    for part in range(count):
        columns = pl.ds(part * span, span)
        copies.append(pltpu.make_async_copy(train.at[:, columns], held.at[:, columns], done.at[part]))
        copies[-1].start()
    each = blocks.shape[1] // count

    def arrive(z):
        if z % each == 0:
            copies[z // each].wait()

    out[...] = scores(blocks, held, arrive).astype(out.dtype)


def there_kernel(blocks, here, train, out):
    chip = lax.axis_index("xh")
    layers, _, rows, _ = out.shape
    there = scores(blocks, train).astype(out.dtype)
    for layer in range(layers):
        piece = slice(layer * rows, (layer + 1) * rows)
        out[layer, chip] = here[piece]
        out[layer, 1 - chip] = there[piece]


def in_vmem(kernel, out_shape, *operands, scratch=(), outside=None, room=40):
    flops = 2 * operands[0].size * operands[-1].shape[0]
    spec = pl.BlockSpec(memory_space=pltpu.VMEM)
    return pl.pallas_call(
        kernel,
        out_shape=out_shape,
        in_specs=[pl.BlockSpec(memory_space=pl.ANY) if i == outside else spec for i in range(len(operands))],
        out_specs=spec,
        scratch_shapes=scratch,
        compiler_params=pltpu.CompilerParams(vmem_limit_bytes=room * 2**20),
        cost_estimate=pl.CostEstimate(flops=flops, bytes_accessed=2**20, transcendentals=0),
    )(*operands)


def on_device(groups, queries, fisher, train_grads):
    width, group = queries.shape[2], queries.shape[1]
    layers, slots = lax.axis_size("layer"), lax.axis_size("z")
    train = train_grads[0]

    mine = fisher[0].T
    fisher_got = lax.ppermute(mine, "xh", SWAP)
    train_got = lax.ppermute(train, "xh", SWAP)

    scaled = in_vmem(scale_kernel, jax.ShapeDtypeStruct((group, width + 128), jnp.float32), queries[0])
    rows = gather_z(scaled.astype(jnp.float16), groups).reshape(slots * group, width + 128)
    rows = lax.all_gather(rows, "c", axis=0, tiled=True)
    rows, fisher_got = lax.optimization_barrier((rows, fisher_got))
    back = jnp.exp2(rows[:, width : width + 1].astype(jnp.float32) - TOP)
    rows = (rows[:, :width].astype(jnp.float32) * back).astype(jnp.bfloat16)

    height, span = slots * 2 * group, 2 * mine.shape[0]
    chunk = in_vmem(
        chunk_kernel,
        jax.ShapeDtypeStruct((height + group, span), jnp.float32),
        rows,
        mine,
        fisher_got,
        scratch=[pltpu.VMEM((height, span), jnp.float32)],
    )
    blocks = lax.all_gather(gather_z(chunk.astype(jnp.float16), groups), "c", axis=0)
    back = jnp.exp2(blocks[:, :, height : height + 1, :1].astype(jnp.float32) - TOP)
    blocks = (blocks[:, :, :height].astype(jnp.float32) * back).astype(jnp.bfloat16)
    here = in_vmem(
        here_kernel,
        jax.ShapeDtypeStruct((height, train.shape[0]), jnp.bfloat16),
        blocks,
        train,
        scratch=[pltpu.VMEM(train.shape, train.dtype), pltpu.SemaphoreType.DMA((4,))],
        outside=1,
        room=51,
    )
    parts_shape = jax.ShapeDtypeStruct((layers, 2, height // layers, train.shape[0]), jnp.bfloat16)
    parts = in_vmem(there_kernel, parts_shape, blocks, here, train_got)

    parts = lax.all_to_all(parts.reshape(2 * layers, height // layers, -1), ("layer", "xh"), 0, 0)
    return in_vmem(sum_kernel, jax.ShapeDtypeStruct((2 * height // layers, parts.shape[2]), jnp.float32), parts)


def solution(mesh):
    layers, spread = mesh.devices.shape
    slots = spread // 4
    fine = Mesh(mesh.devices.reshape(layers, slots, 2, 2), AXES)
    groups = [
        [layer * spread + 4 * z + 2 * chip + (side + z) % 2 for z in range(slots)]
        for layer in range(layers)
        for chip in range(2)
        for side in range(2)
    ]
    ex = ("z", "xh", "c")
    in_specs = (P("layer", ex, None), P("layer", None, ex), P("layer", ex, None))
    return jax.shard_map(
        functools.partial(on_device, groups),
        mesh=fine,
        in_specs=in_specs,
        out_specs=P("layer", ex),
        check_vma=False,
    )
```

```python
import functools

import jax
import jax.numpy as jnp
from jax import lax
from jax.experimental import pallas as pl
from jax.experimental.pallas import tpu as pltpu
from jax.sharding import Mesh, PartitionSpec as P

TOP = 14.0
AXES = ("layer", "z", "xh", "c")
SWAP = [(0, 1), (1, 0)]
NT = (((1,), (1,)), ((), ()))


def exponent_of(peak):
    return jnp.clip(jnp.floor(jnp.log2(jnp.maximum(peak, 1e-37))), -100.0, 100.0)


def gather_z(x, groups):
    return lax.all_gather(x, AXES, axis=0, axis_index_groups=groups)


def core_at(entry, z):
    return lax.rem(entry + lax.axis_index("z") + z, 2)


def columns_of(mine, got):
    first = lax.axis_index("xh") == 0
    return jnp.concatenate([jnp.where(first, mine[...], got[...]), jnp.where(first, got[...], mine[...])], axis=0)


def rounded_product(rows, columns):
    value = lax.dot_general(rows[...], columns, NT, preferred_element_type=jnp.float32)
    return value.astype(jnp.bfloat16).astype(jnp.float32)


def scale_kernel(rows, out):
    value = rows[...].astype(jnp.float32)
    exponent = exponent_of(jnp.max(jnp.abs(value), axis=1, keepdims=True))
    out[:, : value.shape[1]] = value * jnp.exp2(TOP - exponent)
    out[:, value.shape[1] :] = jnp.broadcast_to(exponent, (value.shape[0], 128))


def sum_kernel(parts, out):
    span = out.shape[0] // 4
    for z in range(2):
        for chip in range(2):
            piece = parts[chip, z * span : (z + 1) * span].astype(jnp.float32)
            for layer in range(1, parts.shape[0] // 2):
                piece = piece + parts[2 * layer + chip, z * span : (z + 1) * span].astype(jnp.float32)
            begin = (2 * z + chip) * span
            out[begin : begin + span] = piece


def scale_kernel(rows, out):
    value = rows[...].astype(jnp.float32)
    exponent = exponent_of(jnp.max(jnp.abs(value), axis=1, keepdims=True))
    out[:, : value.shape[1]] = value * jnp.exp2(TOP - exponent)
    out[:, value.shape[1] :] = jnp.broadcast_to(exponent, (value.shape[0], 128))


def sum_kernel(parts, out):
    span = out.shape[0] // 4
    for z in range(2):
        for chip in range(2):
            piece = parts[chip, z * span : (z + 1) * span].astype(jnp.float32)
            for layer in range(1, parts.shape[0] // 2):
                piece = piece + parts[2 * layer + chip, z * span : (z + 1) * span].astype(jnp.float32)
            begin = (2 * z + chip) * span
            out[begin : begin + span] = piece


def near_kernel(rows, mine, got, out):
    out[...] = rounded_product(rows, columns_of(mine, got))


def chunk_kernel(rows, mine, got, out, order):
    product = rounded_product(rows, columns_of(mine, got))
    height = order.shape[0]
    group = out.shape[0] - height
    slots = height // (2 * group)
    for entry in range(2):
        for z in range(slots):
            begin = (entry * slots + z) * group
            place = pl.multiple_of((2 * z + core_at(entry, z)) * group, group)
            order[pl.ds(place, group)] = product[begin : begin + group]
    value = order[...]
    peak = jnp.max(jnp.max(jnp.abs(value), axis=0, keepdims=True), axis=1, keepdims=True)
    exponent = exponent_of(peak)
    tail = jnp.broadcast_to(exponent, (group, out.shape[1]))
    out[...] = jnp.concatenate([value * jnp.exp2(TOP - exponent), tail], axis=0)


def scores(blocks, train, arrive=lambda z: None):
    half = blocks.shape[3] // 2
    total = jnp.zeros((blocks.shape[2], train.shape[0]), jnp.float32)
    for z in range(blocks.shape[1]):
        arrive(z)
        straight = core_at(0, z) == 0
        one = jnp.where(straight, blocks[0, z], blocks[1, z])
        two = jnp.where(straight, blocks[1, z], blocks[0, z])
        left = jnp.concatenate([one[:, :half], two[:, :half], one[:, half:], two[:, half:]], axis=1)
        right = train[:, z * left.shape[1] : (z + 1) * left.shape[1]]
        total = total + lax.dot_general(left, right, NT, preferred_element_type=jnp.float32)
    return total


def here_kernel(blocks, train, out, held, done):
    count = done.shape[0]
    span = train.shape[1] // count
    copies = []
    for part in range(count):
        columns = pl.ds(part * span, span)
        copies.append(pltpu.make_async_copy(train.at[:, columns], held.at[:, columns], done.at[part]))
    each = blocks.shape[1] // count
    for copy in copies[:2]:
        copy.start()

    def arrive(z):
        if z % each == 0:
            copies[z // each].wait()
            for copy in copies[z // each + 2 : z // each + 3]:
                copy.start()

    out[...] = scores(blocks, held, arrive).astype(out.dtype)


def there_kernel(blocks, here, train, out):
    chip = lax.axis_index("xh")
    layers, _, rows, _ = out.shape
    there = scores(blocks, train).astype(out.dtype)
    for layer in range(layers):
        piece = slice(layer * rows, (layer + 1) * rows)
        out[layer, chip] = here[piece]
        out[layer, 1 - chip] = there[piece]


def in_vmem(kernel, out_shape, *operands, scratch=(), outside=None, room=40):
    flops = 2 * operands[0].size * operands[-1].shape[0]
    spec = pl.BlockSpec(memory_space=pltpu.VMEM)
    return pl.pallas_call(
        kernel,
        out_shape=out_shape,
        in_specs=[pl.BlockSpec(memory_space=pl.ANY) if i == outside else spec for i in range(len(operands))],
        out_specs=spec,
        scratch_shapes=scratch,
        compiler_params=pltpu.CompilerParams(vmem_limit_bytes=room * 2**20),
        cost_estimate=pl.CostEstimate(flops=flops, bytes_accessed=2**20, transcendentals=0),
    )(*operands)


def on_device(groups, queries, fisher, train_grads):
    width, group = queries.shape[2], queries.shape[1]
    layers, slots = lax.axis_size("layer"), lax.axis_size("z")
    train = train_grads[0]

    mine = fisher[0].T
    fisher_got = lax.ppermute(mine, "xh", SWAP)
    train_got = lax.ppermute(train, "xh", SWAP)

    scaled = in_vmem(scale_kernel, jax.ShapeDtypeStruct((group, width + 128), jnp.float32), queries[0])
    rows = gather_z(scaled.astype(jnp.float16), groups).reshape(slots * group, width + 128)
    rows = lax.all_gather(rows, "c", axis=0, tiled=True)
    rows, fisher_got = lax.optimization_barrier((rows, fisher_got))
    back = jnp.exp2(rows[:, width : width + 1].astype(jnp.float32) - TOP)
    rows = (rows[:, :width].astype(jnp.float32) * back).astype(jnp.bfloat16)

    height, span = slots * 2 * group, 2 * mine.shape[0]
    chunk = in_vmem(
        chunk_kernel,
        jax.ShapeDtypeStruct((height + group, span), jnp.float32),
        rows,
        mine,
        fisher_got,
        scratch=[pltpu.VMEM((height, span), jnp.float32)],
    )
    blocks = lax.all_gather(gather_z(chunk.astype(jnp.float16), groups), "c", axis=0)
    back = jnp.exp2(blocks[:, :, height : height + 1, :1].astype(jnp.float32) - TOP)
    blocks = (blocks[:, :, :height].astype(jnp.float32) * back).astype(jnp.bfloat16)
    here = in_vmem(
        here_kernel,
        jax.ShapeDtypeStruct((height, train.shape[0]), jnp.bfloat16),
        blocks,
        train,
        scratch=[pltpu.VMEM(train.shape, train.dtype), pltpu.SemaphoreType.DMA((min(8, slots),))],
        outside=1,
        room=51,
    )
    parts_shape = jax.ShapeDtypeStruct((layers, 2, height // layers, train.shape[0]), jnp.bfloat16)
    parts = in_vmem(there_kernel, parts_shape, blocks, here, train_got)

    parts = lax.all_to_all(parts.reshape(2 * layers, height // layers, -1), ("layer", "xh"), 0, 0)
    return in_vmem(sum_kernel, jax.ShapeDtypeStruct((2 * height // layers, parts.shape[2]), jnp.float32), parts)


def solution(mesh):
    layers, spread = mesh.devices.shape
    slots = spread // 4
    fine = Mesh(mesh.devices.reshape(layers, slots, 2, 2), AXES)
    groups = [
        [layer * spread + 4 * z + 2 * chip + (side + z) % 2 for z in range(slots)]
        for layer in range(layers)
        for chip in range(2)
        for side in range(2)
    ]
    ex = ("z", "xh", "c")
    in_specs = (P("layer", ex, None), P("layer", None, ex), P("layer", ex, None))
    return jax.shard_map(
        functools.partial(on_device, groups),
        mesh=fine,
        in_specs=in_specs,
        out_specs=P("layer", ex),
        check_vma=False,
    )
```
